32 devices in a mesh: row: 4 (over x, core), col: 8 (over z, y).
Axes of the slice: x: 2, y: 2, z: 4, core: 2. Of those that a mesh axis runs over, the one named last changes fastest.
Arguments:
- vectors: float32 [2048, 2048], P('row', 'col'), may hold values from -6 to 6
- reflectors: float32 [4, 2048, 256], P(None, ('row', 'col')), may hold values from -6 to 6
- owner_list: int32 [16], replicated, may hold values from 0 to 7, as said below
- slot_list: int32 [16], replicated, may hold values from 0 to 1
Outputs:
- result: float32 [2048, 2048], P('row', 'col')
The draws below stay inside these ranges and needn't reach their ends.
Inputs may be any that keep to these rules, and one draw needn't show every extreme that they name: owner_list * 2 + slot_list takes each value 0 to 15 exactly once.
All inputs are finite; a program needn't handle non-finite values.
Results may differ from the reference program's by a relative error of at most 0.0001.
Values sent between devices are 32-bit elements; how exact they have to be, the bound alone decides.
No kernel may reach another device: no remote copies, remote signals or barrier semaphores. Data moves between devices by JAX's collectives and lax.ppermute only.
A program may use at most 64 MiB of HBM per device.

```python
import jax
import jax.numpy as jnp
from jax import lax

BW = 128
BLK_DEV = 2
NB = 256
PANELS = 4
NROWS = 2048
BLOCKS = 16
NCOLS = 2048


def block_order(key):
    return jax.random.permutation(jax.random.fold_in(key, 7), BLOCKS).astype(jnp.int32)


def draw_owner_list(key, part):
    return block_order(key) // BLK_DEV


def draw_slot_list(key, part):
    return block_order(key) % BLK_DEV


def level_of(key, dims, cuts, least, top_value):
    def one(axis_at, parts):
        heights = jax.random.uniform(jax.random.fold_in(jax.random.fold_in(key, 6), axis_at), (parts,), jnp.float32, least / len(cuts), top_value / len(cuts))
        return jnp.repeat(jnp.exp(heights), dims[axis_at] // parts).reshape((-1,) + (1,) * (len(dims) - axis_at - 1))

    factor_of = one(*cuts[0])
    for cut in cuts[1:]:
        factor_of = factor_of * one(*cut)
    return factor_of


def normal_values(own_key, dims, spread, reach, cuts=(), kind=jnp.bfloat16):
    array = spread * jax.random.normal(own_key, dims, jnp.float32)
    if cuts:
        array = array * level_of(own_key, dims, cuts, -0.22, 0.18)
    return jnp.clip(array, -reach, reach).astype(kind)


def setup_inputs(seed: int = 0) -> dict:
    arg_keys = jax.random.split(jax.random.key(seed), 5)
    return {
        "vectors": normal_values(arg_keys[0], (NROWS, NCOLS), 1.0, 6.0, ((0, 4), (1, 8)), jnp.float32),
        "reflectors": normal_values(arg_keys[1], (PANELS, NROWS, NB), 1.0, 6.0, ((1, 32),), jnp.float32),
        "owner_list": draw_owner_list(jax.random.fold_in(arg_keys[4], 71), 0),
        "slot_list": draw_slot_list(jax.random.fold_in(arg_keys[4], 71), 0),
    }


def reorder(vectors, owner_list, slot_list):
    blocks = owner_list.shape[0]
    target = (owner_list * BLK_DEV + slot_list).astype(jnp.int32)
    inverse = jnp.zeros((blocks,), jnp.int32).at[target].set(jnp.arange(blocks, dtype=jnp.int32))
    blocks_view = vectors.reshape(vectors.shape[0], blocks, BW)
    return jnp.take(blocks_view, inverse, axis=1).reshape(vectors.shape[0], blocks * BW)

def apply_panel(slab_now, panel_rows, gram_sum):
    upper_form = jnp.triu(gram_sum, 1) + jnp.diag(jnp.diagonal(gram_sum) * 0.5)
    product = jnp.dot(panel_rows.T.astype(jnp.float32), slab_now.astype(jnp.float32), precision=lax.Precision.HIGHEST, preferred_element_type=jnp.float32)
    coefficients = lax.linalg.triangular_solve(upper_form, product, left_side=True, lower=False)
    return slab_now - jnp.dot(panel_rows.astype(jnp.float32), coefficients.astype(jnp.float32), precision=lax.Precision.HIGHEST, preferred_element_type=jnp.float32)

def reference(vectors, reflectors, owner_list, slot_list):
    slab_now = reorder(vectors, owner_list, slot_list)
    for panel_index in reversed(range(PANELS)):
        panel_rows = reflectors[panel_index]
        gram_sum = jnp.dot(panel_rows.T.astype(jnp.float32), panel_rows.astype(jnp.float32), precision=lax.Precision.HIGHEST, preferred_element_type=jnp.float32)
        slab_now = apply_panel(slab_now, panel_rows, gram_sum)
    return slab_now
```

```python
import functools

import jax
import jax.numpy as jnp
from jax import lax
from jax.experimental import pallas as pl
from jax.experimental.pallas import tpu as pltpu
from jax.sharding import PartitionSpec as P

BW = 128
BLK_DEV = 2
LOW = 8
F32, BF16 = jnp.float32, jnp.bfloat16
PARAMS = pltpu.CompilerParams(vmem_limit_bytes=48 * 1024 * 1024)


def vmem(count):
    return [pl.BlockSpec(memory_space=pltpu.VMEM)] * count


def smem(count):
    return [pl.BlockSpec(memory_space=pltpu.SMEM)] * count


def halves(value):
    high = value.astype(BF16)
    return high, (value - high.astype(F32)).astype(BF16)


def dot(left, right):
    return jnp.dot(left, right, preferred_element_type=F32)


def dot3(left, right):
    return dot(left[0], right[0]) + (dot(left[0], right[1]) + dot(left[1], right[0]))


def pairs_of(panels):
    return [(p, q) for p in range(panels) for q in range(p + 1, panels)]


def reorder_kernel(half, owner, slot, spread, ordered):
    def move(block, carry):
        place = slot[block] * half + owner[block]
        parity = block % BLK_DEV

        @pl.when(parity == 0)
        def _():
            ordered[place] = spread[block // BLK_DEV, :, :BW]

        @pl.when(parity == 1)
        def _():
            ordered[place] = spread[block // BLK_DEV, :, BW:]

        return carry

    lax.fori_loop(0, ordered.shape[0], move, 0)


def reorder(spread, owner_list, slot_list):
    cols, rows, _ = spread.shape
    return pl.pallas_call(
        functools.partial(reorder_kernel, cols),
        out_shape=jax.ShapeDtypeStruct((cols * BLK_DEV, rows, BW), F32),
        in_specs=smem(2) + vmem(1),
        out_specs=vmem(1)[0],
        compiler_params=PARAMS,
        name="reorder",
    )(owner_list, slot_list, spread)


def gram_kernel(count, has_before, *refs):
    pieces, refs = refs[:count], refs[count:]
    if has_before:
        (diag_before, corner_before), refs = refs[:2], refs[2:]
    high, low, high_t, low_t, diag, corner = refs
    panels, rows, width = pieces[0].shape
    for at, piece in enumerate(pieces):
        for p in range(panels):
            top, rest = halves(piece[p])
            high[at * rows:(at + 1) * rows, p * width:(p + 1) * width] = top
            low[at * rows:(at + 1) * rows, p * width:(p + 1) * width] = rest
    for p in range(panels):
        cut = slice(p * width, (p + 1) * width)
        high_t[cut, :] = high[:, cut].T
        low_t[cut, :] = low[:, cut].T

    def product(p, q):
        left, right = slice(p * width, (p + 1) * width), slice(q * width, (q + 1) * width)
        return dot3((high_t[left, :], low_t[left, :]), (high[:, right], low[:, right]))

    for p in range(panels):
        value = product(p, p)
        diag[p] = value + diag_before[p] if has_before else value
    for at, (p, q) in enumerate(pairs_of(panels)):
        value = product(p, q)
        corner[at] = value + corner_before[at] if has_before else value


def gram(pieces, before):
    panels, rows, width = pieces[0].shape
    count, full = len(pieces), panels * width
    total = count * rows
    corners = len(pairs_of(panels))
    inputs = list(pieces) + list(before or ())
    return pl.pallas_call(
        functools.partial(gram_kernel, count, before is not None),
        out_shape=(
            jax.ShapeDtypeStruct((total, full), BF16),
            jax.ShapeDtypeStruct((total, full), BF16),
            jax.ShapeDtypeStruct((full, total), BF16),
            jax.ShapeDtypeStruct((full, total), BF16),
            jax.ShapeDtypeStruct((panels, width, width), F32),
            jax.ShapeDtypeStruct((corners, width, width), F32),
        ),
        in_specs=vmem(len(inputs)),
        out_specs=tuple(vmem(6)),
        compiler_params=PARAMS,
        cost_estimate=pl.CostEstimate(
            flops=6 * (panels + corners) * width * width * total, bytes_accessed=16 * total * full, transcendentals=0
        ),
        name="gram",
    )(*inputs)


def invert_kernel(own, other, inverse):
    panels, order, _ = own.shape
    row = lax.broadcasted_iota(jnp.int32, (order, order), 0)
    col = lax.broadcasted_iota(jnp.int32, (order, order), 1)
    on_diag, upper = row == col, row < col
    identity = jnp.where(on_diag, 1.0, 0.0).astype(F32)
    strict, scale = [], []
    for p in range(panels):
        gram_sum = own[p] + other[p]
        half = jnp.where(on_diag, 0.5 * gram_sum, 0.0)
        by_row = 1.0 / jnp.sum(half, axis=1, keepdims=True)
        by_col = 1.0 / jnp.sum(half, axis=0, keepdims=True)
        strict.append(jnp.where(upper, gram_sum * by_row, 0.0))
        scale.append(by_col)

    def multiply(left, right):
        return dot3(halves(left), halves(right))

    size = 16
    same = (row // size) == (col // size)
    power = [jnp.where(same, -value, 0.0) for value in strict]
    accum = [identity + value for value in power]
    for _ in range(3):
        power = [multiply(value, value) for value in power]
        accum = [value + multiply(value, extra) for value, extra in zip(accum, power)]
    while size < order:
        wider = (row // (2 * size)) == (col // (2 * size))
        mask = jnp.logical_and(wider, jnp.logical_not((row // size) == (col // size)))
        part = [multiply(value, jnp.where(mask, edge, 0.0)) for value, edge in zip(accum, strict)]
        accum = [value - multiply(edge, value) for value, edge in zip(accum, part)]
        size *= 2
    for p in range(panels):
        inverse[p] = accum[p] * scale[p]


def invert(own, other):
    return pl.pallas_call(
        invert_kernel,
        out_shape=jax.ShapeDtypeStruct(own.shape, F32),
        in_specs=vmem(2),
        out_specs=vmem(1)[0],
        compiler_params=PARAMS,
        cost_estimate=pl.CostEstimate(flops=10**10, bytes_accessed=own.size * 12, transcendentals=0),
        name="invert",
    )(own, other)


def place_of(at, inner):
    row, col = lax.axis_index("row"), lax.axis_index("col")
    group, z = at // 4, at % 4
    outer, low = row // inner, col % LOW
    odd = (row % inner) % 2
    first, second = group & 1, group >> 1
    by_y = jnp.where(odd == 0, first, second)
    by_x = jnp.where(odd == 0, second, first)
    return jnp.bitwise_xor(outer, by_x), jnp.bitwise_xor(low, z * 2 + by_y), by_x


def project_kernel(inner, high_a, low_a, high_b, low_b, slab, product, slab_high, slab_low):
    rows = slab.shape[1]
    for at in range(2 * LOW):
        outer, low, _ = place_of(at, inner)
        high, rest = halves(slab[outer * LOW + low])
        cut = slice(at * rows, (at + 1) * rows)
        slab_high[cut, :BW] = high
        slab_high[cut, BW:] = rest
        slab_low[cut, :] = high
    middle = LOW * rows
    wide = dot(high_a[...], slab_high[:middle, :]) + dot(high_b[...], slab_high[middle:, :])
    narrow = dot(low_a[...], slab_low[:middle, :]) + dot(low_b[...], slab_low[middle:, :])
    product[...] = wide[:, :BW] + (wide[:, BW:] + narrow)


def project(inner, transposed, slab):
    full = transposed[0].shape[0]
    total = slab.shape[0] * slab.shape[1]
    return pl.pallas_call(
        functools.partial(project_kernel, inner),
        out_shape=jax.ShapeDtypeStruct((full, BW), F32),
        in_specs=vmem(5),
        out_specs=vmem(1)[0],
        scratch_shapes=[pltpu.VMEM((total, 2 * BW), BF16), pltpu.VMEM((total, BW), BF16)],
        compiler_params=PARAMS,
        cost_estimate=pl.CostEstimate(flops=8 * full * total * BW, bytes_accessed=4 * total * full, transcendentals=0),
        name="project",
    )(*transposed, slab)


def update_kernel(inner, own, other, inverse, corner_own, corner_other, high_a, low_a, high_b, low_b, slab, result, solved_wide, solved_high):
    panels, width, _ = inverse.shape
    rows = slab.shape[1]
    pairs = pairs_of(panels)
    solved = [None] * panels
    for p in reversed(range(panels)):
        cut = slice(p * width, (p + 1) * width)
        value = own[cut, :] + other[cut, :]
        for at, (i, q) in enumerate(pairs):
            if i == p:
                value = value - dot3(halves(corner_own[at] + corner_other[at]), solved[q])
        value = dot3(halves(inverse[p]), halves(value))
        solved[p] = halves(value)
        solved_wide[cut, :BW] = solved[p][0]
        solved_wide[cut, BW:] = solved[p][1]
        solved_high[cut, :] = solved[p][0]
    for part, (high, low) in enumerate(((high_a, low_a), (high_b, low_b))):
        wide = dot(high[...], solved_wide[...])
        change = wide[:, :BW] + (wide[:, BW:] + dot(low[...], solved_high[...]))
        for at in range(LOW):
            outer, low_at, away = place_of(part * LOW + at, inner)
            result[away, low_at] = slab[outer * LOW + low_at] - change[at * rows:(at + 1) * rows, :]


def update(inner, own, other, inverse, corner_own, corner_other, straight, slab):
    full = own.shape[0]
    return pl.pallas_call(
        functools.partial(update_kernel, inner),
        out_shape=jax.ShapeDtypeStruct((2, LOW) + slab.shape[1:], F32),
        in_specs=vmem(10),
        out_specs=vmem(1)[0],
        scratch_shapes=[pltpu.VMEM((full, 2 * BW), BF16), pltpu.VMEM((full, BW), BF16)],
        compiler_params=PARAMS,
        name="update",
    )(own, other, inverse, corner_own, corner_other, *straight, slab)


def on_device(rows, cols, vectors, reflectors, owner_list, slot_list):
    inner = rows // 2
    extra = cols // LOW
    local_rows = vectors.shape[0] // cols

    def at(row, col):
        return row * cols + col

    def send(value, change):
        perm = [(at(r, c), at(*change(r, c))) for r in range(rows) for c in range(cols)]
        return lax.ppermute(value, ("row", "col"), perm)

    def by_z(step):
        return lambda r, c: (r, c ^ (2 * step))

    def by_first(r, c):
        return (r, c ^ 1) if (r % inner) % 2 == 0 else ((r + inner) % rows, c)

    def by_second(r, c):
        return (r, c ^ 1) if (r % inner) % 2 == 1 else ((r + inner) % rows, c)

    own = reflectors
    if extra > 1:
        groups = [[e * LOW + low for e in range(extra)] for low in range(LOW)]
        own = lax.all_gather(own, "col", axis=1, tiled=True, axis_index_groups=groups)
    start = [own] + [send(own, by_z(step)) for step in (1, 2, 3)]
    spread = lax.all_to_all(vectors.reshape(cols, local_rows, -1), "col", split_axis=0, concat_axis=0, tiled=True)
    first = [send(piece, by_first) for piece in start]
    second = [send(piece, by_second) for piece in start + first]

    ordered = reorder(spread, owner_list, slot_list)
    groups = [[at(o * inner + i, c) for o in range(2) for c in range(cols)] for i in range(inner)]
    slab = lax.all_to_all(ordered, ("row", "col"), split_axis=0, concat_axis=0, tiled=True, axis_index_groups=groups)
    slab = slab.reshape(2, extra, LOW, local_rows, BW).transpose(0, 2, 1, 3, 4)
    slab = slab.reshape(2 * LOW, extra * local_rows, BW)

    high_a, low_a, high_at, low_at, diag, corner = gram(start + first, None)
    high_b, low_b, high_bt, low_bt, diag, corner = gram(second, (diag, corner))
    product = project(inner, (high_at, low_at, high_bt, low_bt), slab)

    def over_inner(value, bit):
        return send(value, lambda r, c: (r ^ bit, c))

    bit = 1
    while 2 * bit < inner:
        diag, corner, product = (value + over_inner(value, bit) for value in (diag, corner, product))
        bit *= 2
    inverse = invert(diag, over_inner(diag, bit))
    result = update(
        inner, product, over_inner(product, bit), inverse, corner, over_inner(corner, bit), (high_a, low_a, high_b, low_b), slab
    )

    keep, away = result[0], result[1]
    back = send(away, lambda r, c: ((r + inner) % rows, c))
    outer = lax.axis_index("row") // inner

    def natural(value):
        return value.reshape(LOW, extra, local_rows, BW).transpose(1, 0, 2, 3).reshape(vectors.shape[0], BW)

    keep, back = natural(keep), natural(back)
    is_first = outer == 0
    return jnp.concatenate([jnp.where(is_first, keep, back), jnp.where(is_first, back, keep)], axis=1)


def solution(mesh):
    return jax.shard_map(
        functools.partial(on_device, mesh.shape["row"], mesh.shape["col"]),
        mesh=mesh,
        in_specs=(P("row", "col"), P(None, ("row", "col"), None), P(), P()),
        out_specs=P("row", "col"),
        check_vma=False,
    )
```

```python
import functools

import jax
import jax.numpy as jnp
from jax import lax
from jax.experimental import pallas as pl
from jax.experimental.pallas import tpu as pltpu
from jax.sharding import PartitionSpec as P

BW = 128
BLK_DEV = 2
LOW = 8
CHUNKS = 4
F32, BF16 = jnp.float32, jnp.bfloat16


def vmem(count):
    return [pl.BlockSpec(memory_space=pltpu.VMEM)] * count


def smem(count):
    return [pl.BlockSpec(memory_space=pltpu.SMEM)] * count


def shape(dims, kind=F32):
    return jax.ShapeDtypeStruct(tuple(dims), kind)


def call(body, name, outs, inputs, scratch=(), scalars=0, far=0, far_outs=0, copies=0, aliases=None, flops=0, mib=16, near_pinned=False):
    near = len(inputs) - scalars - far
    any_space = pl.BlockSpec(memory_space=pl.ANY)
    return pl.pallas_call(
        body,
        out_shape=tuple(pltpu.VMEM(out.shape, out.dtype) if near_pinned else out for out in outs[:len(outs) - far_outs]) + tuple(pltpu.HBM(out.shape, out.dtype) for out in outs[len(outs) - far_outs:]),
        in_specs=smem(scalars) + vmem(near) + [any_space] * far,
        out_specs=tuple(vmem(len(outs) - far_outs) + [any_space] * far_outs),
        scratch_shapes=list(scratch) + ([pltpu.SemaphoreType.DMA((copies,))] if copies else []),
        input_output_aliases=aliases or {},
        compiler_params=pltpu.CompilerParams(vmem_limit_bytes=mib * 1024 * 1024),
        cost_estimate=pl.CostEstimate(flops=flops, bytes_accessed=4 * 1024 * 1024, transcendentals=0),
        name=name,
    )(*inputs)


def pinned(arrays):
    return [pltpu.with_memory_space_constraint(array, pltpu.HBM) for array in arrays]


def start_copies(pairs, sems, base=0):
    copies = [pltpu.make_async_copy(src, dst, sems.at[base + at]) for at, (src, dst) in enumerate(pairs)]
    for copy in copies:
        copy.start()
    return copies


def halves(value):
    high = value.astype(BF16)
    return high, (value - high.astype(F32)).astype(BF16)


def dot(left, right):
    return jnp.dot(left, right, preferred_element_type=F32)


def dot3(left, right):
    return dot(left[0], right[0]) + (dot(left[0], right[1]) + dot(left[1], right[0]))


def pairs_of(panels):
    return [(p, q) for p in range(panels) for q in range(p + 1, panels)]


def reorder_kernel(half, owner_list, slot_list, spread, ordered, owner, slot, held, sems):
    copies = start_copies([(owner_list, owner), (slot_list, slot), (spread, held)], sems)
    for copy in copies:
        copy.wait()

    def move(block, carry):
        place = slot[block] * half + owner[block]
        parity = block % BLK_DEV

        @pl.when(parity == 0)
        def _():
            ordered[place] = held[block // BLK_DEV, :, :BW]

        @pl.when(parity == 1)
        def _():
            ordered[place] = held[block // BLK_DEV, :, BW:]

        return carry

    lax.fori_loop(0, ordered.shape[0], move, 0)


def reorder(spread, owner_list, slot_list):
    cols, rows, _ = spread.shape
    outs = [shape((cols * BLK_DEV, rows, BW))]
    scratch = [pltpu.SMEM(owner_list.shape, jnp.int32), pltpu.SMEM(slot_list.shape, jnp.int32), pltpu.VMEM(spread.shape, F32)]
    return call(
        functools.partial(reorder_kernel, cols), "reorder", outs, (owner_list, slot_list, spread), far=3, copies=3, scratch=scratch
    )[0]


def is_odd(inner):
    return (lax.axis_index("row") % inner) % 2


def gram_kernel(inner, count, before, *refs):
    pieces, refs = refs[:4 * count], refs[4 * count:]
    diag, corner, high_out, low_out, staged, high, low, high_t, low_t, sems = refs
    panels, rows, width = pieces[0].shape
    odd = is_odd(inner)
    places = (0, jnp.where(odd == 0, 1, 2), jnp.where(odd == 0, 2, 1), 3)
    arriving = start_copies([(piece, staged.at[at]) for at, piece in enumerate(pieces)], sems)
    for at, copy in enumerate(arriving):
        copy.wait()
        cut = pl.ds(pl.multiple_of((at // 4 * 4 + places[at % 4]) * rows, rows), rows)
        for p in range(panels):
            top, rest = halves(staged[at, p])
            high[cut, p * width:(p + 1) * width] = top
            low[cut, p * width:(p + 1) * width] = rest
    leaving = start_copies([(high, high_out), (low, low_out)], sems, 4 * count)
    cuts = [slice(p * width, (p + 1) * width) for p in range(panels)]
    for p, cut in enumerate(cuts):
        high_t[cut, :] = high[:, cut].T
        low_t[cut, :] = low[:, cut].T
        value = dot3((high_t[cut, :], low_t[cut, :]), (high[:, cut], low[:, cut]))
        diag[p] = value + before[0][p] if before else value
    for at, (p, q) in enumerate(pairs_of(panels)):
        value = dot3((high_t[cuts[p], :], low_t[cuts[p], :]), (high[:, cuts[q]], low[:, cuts[q]]))
        corner[at] = value + before[1][at] if before else value
    for copy in leaving:
        copy.wait()


def gram(inner, pieces, before, after):
    panels, rows, width = pieces[0].shape
    count = len(pieces) // 4
    total, full = len(pieces) * rows, panels * width
    corners = len(pairs_of(panels))
    outs = [shape((panels, width, width)), shape((corners, width, width)), shape((total, full), BF16), shape((total, full), BF16)]
    near = [pltpu.with_memory_space_constraint(array, pltpu.VMEM) for array in before or ()]
    far = list(pieces) + ([] if after is None else [after])

    def body(*refs):
        if near:
            gram_kernel(inner, count, refs[:2], *refs[2:])
        else:
            gram_kernel(inner, count, (), *refs)

    if after is not None and not near:
        body_first = body
        body = lambda *refs: body_first(*refs[:4 * count], *refs[4 * count + 1:])
    return call(
        body, "gram", outs, (*near, *far), far=len(far), far_outs=2, copies=4 * count + 2, aliases={0: 0, 1: 1} if near else None,
        scratch=[
            pltpu.VMEM((len(pieces), panels, rows, width), F32), pltpu.VMEM((total, full), BF16), pltpu.VMEM((total, full), BF16),
            pltpu.VMEM((full, total), BF16), pltpu.VMEM((full, total), BF16),
        ],
        flops=6 * (panels + corners) * width * width * total, mib=32, near_pinned=True,
    )


def invert_kernel(own, other, inverse):
    panels, order, _ = own.shape
    row = lax.broadcasted_iota(jnp.int32, (order, order), 0)
    col = lax.broadcasted_iota(jnp.int32, (order, order), 1)
    on_diag, upper = row == col, row < col
    identity = jnp.where(on_diag, 1.0, 0.0).astype(F32)
    strict, scale = [], []
    for p in range(panels):
        gram_sum = own[p] + other[p]
        half = jnp.where(on_diag, 0.5 * gram_sum, 0.0)
        by_row = 1.0 / jnp.sum(half, axis=1, keepdims=True)
        by_col = 1.0 / jnp.sum(half, axis=0, keepdims=True)
        strict.append(jnp.where(upper, gram_sum * by_row, 0.0))
        scale.append(by_col)

    def multiply(left, right):
        return dot3(halves(left), halves(right))

    size = 16
    same = (row // size) == (col // size)
    power = [jnp.where(same, -value, 0.0) for value in strict]
    accum = [identity + value for value in power]
    for _ in range(3):
        power = [multiply(value, value) for value in power]
        accum = [value + multiply(value, extra) for value, extra in zip(accum, power)]
    while size < order:
        wider = (row // (2 * size)) == (col // (2 * size))
        mask = jnp.logical_and(wider, jnp.logical_not((row // size) == (col // size)))
        uppers = [jnp.concatenate([v[k:k + size] for k in range(0, order, 2 * size)], axis=0) for v in accum]
        part = [multiply(value, jnp.where(mask, edge, 0.0)) for value, edge in zip(uppers, strict)]
        uppers = [u - multiply(edge, value) for u, edge, value in zip(uppers, part, accum)]
        accum = [
            jnp.concatenate(
                [x for k in range(order // (2 * size)) for x in (u[k * size:(k + 1) * size], v[(2 * k + 1) * size:(2 * k + 2) * size])],
                axis=0,
            )
            for u, v in zip(uppers, accum)
        ]
        size *= 2
    for p in range(panels):
        inverse[p] = accum[p] * scale[p]


def invert(own, other):
    own, other = (pltpu.with_memory_space_constraint(value, pltpu.VMEM) for value in (own, other))
    return call(invert_kernel, "invert", [shape(own.shape)], (own, other), flops=5 * 10**9, near_pinned=True)[0]


def place_of(inner, chunk, by_x, by_y):
    row, col = lax.axis_index("row"), lax.axis_index("col")
    return jnp.bitwise_xor(row // inner, by_x), jnp.bitwise_xor(col % LOW, chunk * 2 + by_y)


def project_kernel(inner, parts, *refs):
    arrays, (slab, product, left, held, held_slab, sems) = refs[:len(parts) * 2], refs[len(parts) * 2:]
    rows = slab.shape[1]
    chunk_rows = 4 * rows
    pairs, at = [(slab, held_slab)], 0
    for part, chunks in enumerate(parts):
        for chunk in range(chunks):
            cut = slice(chunk * chunk_rows, (chunk + 1) * chunk_rows)
            pairs += [(arrays[2 * part + k].at[cut, :], held.at[k, at]) for k in range(2)]
            at += 1
    copies = start_copies(pairs, sems)
    copies[0].wait()
    total = None
    for chunk in range(CHUNKS):
        for at in range(4):
            outer, low = place_of(inner, chunk, at // 2, at % 2)
            left[:, at * rows:(at + 1) * rows] = held_slab[outer * LOW + low].T
        high, rest = halves(left[...])
        copies[1 + 2 * chunk].wait()
        copies[2 + 2 * chunk].wait()
        value = dot(high, held[0, chunk]) + (dot(high, held[1, chunk]) + dot(rest, held[0, chunk]))
        total = value if total is None else total + value
    product[...] = total


def project(inner, arrays, slab):
    full = arrays[0].shape[1]
    parts = [array.shape[0] // (4 * slab.shape[1]) for array in arrays[::2]]
    total = 4 * slab.shape[1]
    return call(
        functools.partial(project_kernel, inner, parts), "project", [shape((BW, full))], (*pinned(arrays), slab), far=len(arrays) + 1,
        scratch=[pltpu.VMEM((BW, total), F32), pltpu.VMEM((2, CHUNKS, total, full), BF16), pltpu.VMEM(slab.shape, F32)],
        copies=2 * CHUNKS + 1, flops=6 * full * total * CHUNKS * BW,
    )[0]


def copies_of_half(by_x, parts, arrays, rows, held):
    pairs, at = [], 0
    for part, chunks in enumerate(parts):
        for chunk in range(chunks):
            cut = slice((4 * chunk + 2 * by_x) * rows, (4 * chunk + 2 * by_x + 2) * rows)
            pairs += [(arrays[2 * part + k].at[cut, :], held.at[k, at]) for k in range(2)]
            at += 1
    return pairs


def change(inner, by_x, chunk, held, wide, slab, result):
    rows = slab.shape[1]
    main = dot(held[0, chunk], wide[...])
    delta = main[:, :BW] + (main[:, BW:] + dot(held[1, chunk], wide[:, :BW]))
    for by_y in range(2):
        outer, low_at = place_of(inner, chunk, by_x, by_y)
        result[low_at] = slab[outer * LOW + low_at] - delta[by_y * rows:(by_y + 1) * rows, :]


def solve_kernel(inner, parts, own, other, inverse, *refs):
    (corner_own, corner_other), refs = refs[:2], refs[2:]
    arrays, (slab, away, wide, held_own, held_other, held, held_slab, sems) = refs[:len(parts) * 2], refs[len(parts) * 2:]
    panels, width, _ = inverse.shape
    pairs = pairs_of(panels)
    copies = start_copies(
        [(corner_own, held_own), (corner_other, held_other), (slab, held_slab)] + copies_of_half(1, parts, arrays, slab.shape[1], held), sems
    )
    solved = [None] * panels
    for p in reversed(range(panels)):
        cut = slice(p * width, (p + 1) * width)
        value = (own[:, cut] + other[:, cut]).T
        if p == panels - 2:
            copies[0].wait()
            copies[1].wait()
        for at, (i, q) in enumerate(pairs):
            if i == p:
                value = value - dot3(halves(held_own[at] + held_other[at]), solved[q])
        value = dot3(halves(inverse[p]), halves(value))
        solved[p] = halves(value)
        wide[cut, :BW] = solved[p][0]
        wide[cut, BW:] = solved[p][1]
    copies[2].wait()
    for chunk in range(CHUNKS):
        copies[3 + 2 * chunk].wait()
        copies[4 + 2 * chunk].wait()
        change(inner, 1, chunk, held, wide, held_slab, away)


def keep_kernel(inner, parts, wide, *refs):
    arrays, (slab, keep, held, held_slab, sems) = refs[:len(parts) * 2], refs[len(parts) * 2:]
    copies = start_copies([(slab, held_slab)] + copies_of_half(0, parts, arrays, slab.shape[1], held), sems)
    copies[0].wait()
    for chunk in range(CHUNKS):
        copies[1 + 2 * chunk].wait()
        copies[2 + 2 * chunk].wait()
        change(inner, 0, chunk, held, wide, held_slab, keep)


def on_device(rows, cols, vectors, reflectors, owner_list, slot_list):
    inner = rows // 2
    extra = cols // LOW
    local_rows = vectors.shape[0] // cols
    panels = reflectors.shape[0]

    def at(row, col):
        return row * cols + col

    def send(value, change_of):
        perm = [(at(r, c), at(*change_of(r, c))) for r in range(rows) for c in range(cols)]
        return lax.ppermute(value, ("row", "col"), perm)

    def by_z(step):
        return lambda r, c: (r, c ^ (2 * step))

    def by_first(r, c):
        return (r, c ^ 1) if (r % inner) % 2 == 0 else ((r + inner) % rows, c)

    def by_second(r, c):
        return (r, c ^ 1) if (r % inner) % 2 == 1 else ((r + inner) % rows, c)

    own = reflectors
    if extra > 1:
        groups = [[e * LOW + low for e in range(extra)] for low in range(LOW)]
        own = lax.all_gather(own, "col", axis=1, tiled=True, axis_index_groups=groups)
    def after(value, *others):
        return lax.optimization_barrier((value, *others))[0]

    start = [own, send(own, by_z(1)), send(own, by_z(2))]
    start.append(send(start[2], by_z(1)))
    first, second, both = [], [], []
    first.append(send(start[0], by_first))
    second.append(send(start[0], by_second))
    both.append(send(first[0], by_second))
    first.append(send(start[1], by_first))
    second.append(send(start[1], by_second))
    both.append(send(first[1], by_second))
    vectors = after(vectors, start[1], start[2], first[0], second[0])
    spread = lax.all_to_all(vectors.reshape(cols, local_rows, -1), "col", split_axis=0, concat_axis=0, tiled=True)
    ordered = reorder(spread, owner_list, slot_list)
    first.append(send(start[2], by_first))
    second.append(send(start[2], by_second))
    both.append(send(first[2], by_second))
    first.append(send(start[3], by_first))
    second.append(send(start[3], by_second))
    both.append(send(first[3], by_second))
    groups = [[at(o * inner + i, c) for o in range(2) for c in range(cols)] for i in range(inner)]
    slab = lax.all_to_all(ordered, ("row", "col"), split_axis=0, concat_axis=0, tiled=True, axis_index_groups=groups)
    slab = slab.reshape(2, extra, LOW, local_rows, BW).transpose(0, 2, 1, 3, 4)
    slab = slab.reshape(2 * LOW, extra * local_rows, BW)

    pieces = [(start[chunk], first[chunk], second[chunk], both[chunk]) for chunk in range(CHUNKS)]
    parts = (3, 1)
    arrays, sums = (), None
    *sums, high, low = gram(inner, sum(pieces[0:3], ()), None, ordered)
    arrays += (high, low)
    *sums, high, low = gram(inner, sum(pieces[3:4], ()), sums, None)
    arrays += (high, low)
    diag, corner = sums

    def over_inner(value, bit):
        return send(value, lambda r, c: (r ^ bit, c))

    bits = [1 << k for k in range(inner.bit_length() - 1)]
    for bit in bits[:-1]:
        diag, corner = (value + over_inner(value, bit) for value in (diag, corner))
    bit = bits[-1]
    diag_other = over_inner(diag, bit)
    inverse = invert(diag, diag_other)
    product = project(inner, arrays, slab)
    for step in bits[:-1]:
        product = product + over_inner(product, step)
    full, half_rows, block = product.shape[1], 2 * slab.shape[1], shape((LOW,) + slab.shape[1:])
    half_held = [pltpu.VMEM((2, CHUNKS, half_rows, full), BF16), pltpu.VMEM(slab.shape, F32)]
    away, wide = call(
        functools.partial(solve_kernel, inner, parts), "solve", [block, shape((full, 2 * BW), BF16)],
        (product, over_inner(product, bit), inverse, corner, over_inner(corner, bit), *pinned(arrays), slab),
        far=len(arrays) + 3, copies=2 * CHUNKS + 3, scratch=[pltpu.VMEM(corner.shape, F32)] * 2 + half_held, flops=3 * 10**9,
    )
    back = send(away, lambda r, c: ((r + inner) % rows, c))
    keep, = call(
        functools.partial(keep_kernel, inner, parts), "keep", [block], (wide, *pinned(arrays), slab),
        far=len(arrays) + 1, copies=2 * CHUNKS + 1, scratch=half_held, flops=10**9,
    )
    outer = lax.axis_index("row") // inner

    def natural(value):
        return value.reshape(LOW, extra, local_rows, BW).transpose(1, 0, 2, 3).reshape(vectors.shape[0], BW)

    keep, back = natural(keep), natural(back)
    is_first = outer == 0
    return jnp.concatenate([jnp.where(is_first, keep, back), jnp.where(is_first, back, keep)], axis=1)


def solution(mesh):
    return jax.shard_map(
        functools.partial(on_device, mesh.shape["row"], mesh.shape["col"]),
        mesh=mesh,
        in_specs=(P("row", "col"), P(None, ("row", "col"), None), P(), P()),
        out_specs=P("row", "col"),
        check_vma=False,
    )
```

```python
import functools

import jax
import jax.numpy as jnp
from jax import lax
from jax.experimental import pallas as pl
from jax.experimental.pallas import tpu as pltpu
from jax.sharding import PartitionSpec as P

BW = 128
BLK_DEV = 2
LOW = 8
CHUNKS = 4
F32, BF16 = jnp.float32, jnp.bfloat16


def vmem(count):
    return [pl.BlockSpec(memory_space=pltpu.VMEM)] * count


def smem(count):
    return [pl.BlockSpec(memory_space=pltpu.SMEM)] * count


def shape(dims, kind=F32):
    return jax.ShapeDtypeStruct(tuple(dims), kind)


def call(body, name, outs, inputs, scratch=(), scalars=0, far=0, far_outs=0, copies=0, aliases=None, flops=0, mib=16):
    near = len(inputs) - scalars - far
    any_space = pl.BlockSpec(memory_space=pl.ANY)
    return pl.pallas_call(
        body,
        out_shape=tuple(outs[:len(outs) - far_outs]) + tuple(pltpu.HBM(out.shape, out.dtype) for out in outs[len(outs) - far_outs:]),
        in_specs=smem(scalars) + vmem(near) + [any_space] * far,
        out_specs=tuple(vmem(len(outs) - far_outs) + [any_space] * far_outs),
        scratch_shapes=list(scratch) + ([pltpu.SemaphoreType.DMA((copies,))] if copies else []),
        input_output_aliases=aliases or {},
        compiler_params=pltpu.CompilerParams(vmem_limit_bytes=mib * 1024 * 1024),
        cost_estimate=pl.CostEstimate(flops=flops, bytes_accessed=4 * 1024 * 1024, transcendentals=0),
        name=name,
    )(*inputs)


def pinned(arrays):
    return [pltpu.with_memory_space_constraint(array, pltpu.HBM) for array in arrays]


def start_copies(pairs, sems, base=0):
    copies = [pltpu.make_async_copy(src, dst, sems.at[base + at]) for at, (src, dst) in enumerate(pairs)]
    for copy in copies:
        copy.start()
    return copies


def halves(value):
    high = value.astype(BF16)
    return high, (value - high.astype(F32)).astype(BF16)


def dot(left, right):
    return jnp.dot(left, right, preferred_element_type=F32)


def dot3(left, right):
    rows = left[0].shape[0]
    both = dot(jnp.concatenate(left, axis=0), right[0])
    return both[:rows] + (both[rows:] + dot(left[0], right[1]))


def dot3_wide(left, wide):
    rows = left.shape[0] // 2
    full = dot(left, wide)
    return full[:rows, :BW] + (full[:rows, BW:] + full[rows:, :BW])


def pairs_of(panels):
    return [(p, q) for p in range(panels) for q in range(p + 1, panels)]


def reorder_kernel(half, owner_list, slot_list, spread, ordered, owner, slot, held, sems):
    copies = start_copies([(owner_list, owner), (slot_list, slot), (spread, held)], sems)
    for copy in copies:
        copy.wait()

    def move(block, carry):
        place = slot[block] * half + owner[block]
        parity = block % BLK_DEV

        @pl.when(parity == 0)
        def _():
            ordered[place] = held[block // BLK_DEV, :, :BW]

        @pl.when(parity == 1)
        def _():
            ordered[place] = held[block // BLK_DEV, :, BW:]

        return carry

    lax.fori_loop(0, ordered.shape[0], move, 0)


def reorder(spread, owner_list, slot_list):
    cols, rows, _ = spread.shape
    outs = [shape((cols * BLK_DEV, rows, BW))]
    scratch = [pltpu.SMEM(owner_list.shape, jnp.int32), pltpu.SMEM(slot_list.shape, jnp.int32), pltpu.VMEM(spread.shape, F32)]
    return call(
        functools.partial(reorder_kernel, cols), "reorder", outs, (*pinned((owner_list, slot_list)), spread), far=3, copies=3, scratch=scratch
    )[0]


def is_odd(inner):
    return (lax.axis_index("row") % inner) % 2


def gram_kernel(inner, count, summed, wanted, *refs):
    pieces, refs = refs[:4 * count], refs[4 * count:]
    before, refs = (refs[:len(wanted)], refs[len(wanted):]) if summed else ((), refs)
    outs, (high_out, low_out, staged, high, low, high_t, low_t, *held, sems) = refs[:len(wanted)], refs[len(wanted):]
    panels, rows, width = pieces[0].shape
    odd = is_odd(inner)
    places = (0, jnp.where(odd == 0, 1, 2), jnp.where(odd == 0, 2, 1), 3)
    arriving = start_copies([(piece, staged.at[at]) for at, piece in enumerate(pieces)], sems)
    base = 4 * count
    sums = start_copies(list(zip(before, held)), sems, base)
    for at, copy in enumerate(arriving):
        copy.wait()
        cut = pl.ds(pl.multiple_of((at // 4 * 4 + places[at % 4]) * rows, rows), rows)
        for p in range(panels):
            top, rest = halves(staged[at, p])
            high[cut, p * width:(p + 1) * width] = top
            low[cut, p * width:(p + 1) * width] = rest
    leaving = start_copies([(high, high_out), (low, low_out)], sems, base + 2)
    for copy in sums:
        copy.wait()
    cuts = [slice(p * width, (p + 1) * width) for p in range(panels)]
    for cut in cuts:
        high_t[cut, :] = high[:, cut].T
        low_t[cut, :] = low[:, cut].T
    base += 4
    for kind, blocks in enumerate(wanted):
        for at, (p, q) in enumerate(blocks):
            value = dot3((high_t[cuts[p], :], low_t[cuts[p], :]), (high[:, cuts[q]], low[:, cuts[q]]))
            held[kind][at] = value + held[kind][at] if summed else value
            leaving += start_copies([(held[kind].at[at], outs[kind].at[at])], sems, base)
            base += 1
    for copy in leaving:
        copy.wait()


def diag_pairs(panels):
    return [(p, p) for p in range(panels)]


def gram(inner, pieces, before, wanted, after=None):
    panels, rows, width = pieces[0].shape
    count = len(pieces) // 4
    total, full = len(pieces) * rows, panels * width
    blocks = [shape((len(pairs), width, width)) for pairs in wanted]
    outs = blocks + [shape((total, full), BF16), shape((total, full), BF16)]
    far = list(pieces) + pinned(before or ())
    used = len(far)
    if after is not None:
        far.append(after)

    def body(*refs):
        gram_kernel(inner, count, before is not None, wanted, *refs[:used], *refs[len(far):])

    number = sum(len(pairs) for pairs in wanted)
    return call(
        body, "gram", outs, far, far=len(far), far_outs=len(outs), copies=4 * count + 4 + number,
        scratch=[
            pltpu.VMEM((len(pieces), panels, rows, width), F32), pltpu.VMEM((total, full), BF16), pltpu.VMEM((total, full), BF16),
            pltpu.VMEM((full, total), BF16), pltpu.VMEM((full, total), BF16), *(pltpu.VMEM(block.shape, F32) for block in blocks),
        ],
        flops=6 * number * width * width * total, mib=32,
    )


def corner_kernel(panels, high_in, low_in, before, corner, high, low, held, sems):
    width = high.shape[1] // panels
    copies = start_copies([(high_in, high), (low_in, low), (before, held)], sems)
    for copy in copies[:2]:
        copy.wait()
    cuts = [slice(p * width, (p + 1) * width) for p in range(panels)]
    left = [(high[:, cut].T, low[:, cut].T) for cut in cuts[:-1]]
    copies[2].wait()
    leaving = []
    for at, (p, q) in enumerate(pairs_of(panels)):
        held[at] += dot3(left[p], (high[:, cuts[q]], low[:, cuts[q]]))
        leaving += start_copies([(held.at[at], corner.at[at])], sems, 3 + at)
    for copy in leaving:
        copy.wait()


def corners(panels, parts, before):
    total, full = parts[0].shape
    count, width, _ = before.shape
    return call(
        functools.partial(corner_kernel, panels), "corner", [shape(before.shape)], pinned((*parts, before)), far=3, far_outs=1,
        copies=3 + count, scratch=[pltpu.VMEM((total, full), BF16), pltpu.VMEM((total, full), BF16), pltpu.VMEM(before.shape, F32)],
        flops=6 * count * width * width * total,
    )[0]


def inverses(own, other, copies):
    panels, order, _ = own.shape
    row = lax.broadcasted_iota(jnp.int32, (order, order), 0)
    col = lax.broadcasted_iota(jnp.int32, (order, order), 1)
    apart = jnp.bitwise_xor(row, col)
    strict, edges, scale = [], [], []
    for p in range(panels):
        copies[2 * p].wait()
        copies[2 * p + 1].wait()
        gram_sum = own[p] + other[p]
        half = jnp.where(apart == 0, 0.5 * gram_sum, 0.0)
        by_row = 1.0 / jnp.sum(half, axis=1, keepdims=True)
        by_col = 1.0 / jnp.sum(half, axis=0, keepdims=True)
        strict.append(jnp.where(row < col, gram_sum * by_row, 0.0))
        edges.append(halves(strict[-1]))
        scale.append(by_col)

    def stacked(value):
        high, rest = halves(value)
        return jnp.concatenate([high.astype(F32), rest.astype(F32)], axis=0).astype(BF16)

    def multiply(left, right):
        rows = left.shape[0]
        if rows >= 16:
            return dot3(halves(left), right)
        both = stacked(left)
        full = dot(both, right[0])
        return full[:rows] + (full[rows:] + dot(both, right[1])[:rows])

    def inside(size):
        return jnp.where(apart < size, 1.0, 0.0)

    def widen(value):
        size = value.shape[0]
        if size < 16:
            return halves(jnp.concatenate([value] * (order // size), axis=0) * inside(size))
        mask = inside(size).astype(BF16)
        return tuple(jnp.concatenate([part] * (order // size), axis=0) * mask for part in halves(value))

    size = 8
    mask = inside(size)
    small_row = lax.broadcasted_iota(jnp.int32, (size, order), 0)
    small_col = lax.broadcasted_iota(jnp.int32, (size, order), 1)
    identity = jnp.where(small_row == small_col % size, 1.0, 0.0)
    full = [value * -mask for value in strict]
    power = [sum(value[k:k + size] for k in range(0, order, size)) for value in full]
    accum = [identity + value for value in power]
    power = [multiply(value, halves(wide)) for value, wide in zip(power, full)]
    both = [multiply(jnp.concatenate([value, extra], axis=0), widen(extra)) for value, extra in zip(accum, power)]
    accum = [value + extra[:size] for value, extra in zip(accum, both)]
    accum = [value + multiply(value, widen(extra[size:])) for value, extra in zip(accum, both)]
    while size < order:
        between = (inside(2 * size) - inside(size)).astype(BF16)
        lane = lax.broadcasted_iota(jnp.int32, (size, order), 1)
        even = (lane // size) % 2 == 0
        uppers = [jnp.where(even, value, 0.0) for value in accum]
        part = [multiply(value, (edge[0] * between, edge[1] * between)) for value, edge in zip(uppers, edges)]
        part = [multiply(edge, widen(value)) for edge, value in zip(part, accum)]
        accum = [
            jnp.concatenate([upper - edge, jnp.where(even, 0.0, value)], axis=0) for upper, edge, value in zip(uppers, part, accum)
        ]
        size *= 2
    return [jnp.concatenate(halves(value * by_col), axis=0) for value, by_col in zip(accum, scale)]


def place_of(inner, chunk, by_x, by_y):
    row, col = lax.axis_index("row"), lax.axis_index("col")
    return jnp.bitwise_xor(row // inner, by_x), jnp.bitwise_xor(col % LOW, chunk * 2 + by_y)


def copies_of_rows(parts, arrays, first, count, stride, held):
    pairs = []
    for k in range(2):
        at = k * CHUNKS * count
        for part, chunks in enumerate(parts):
            for chunk in range(chunks):
                pairs.append((arrays[2 * part + k].at[chunk * stride + first:chunk * stride + first + count, :], held.at[at:at + count, :]))
                at += count
    return pairs


def project_kernel(inner, parts, *refs):
    arrays, (slab, product, left, held, held_slab, sems) = refs[:len(parts) * 2], refs[len(parts) * 2:]
    rows = slab.shape[1]
    total = CHUNKS * 4 * rows
    copies = start_copies([(slab, held_slab)] + copies_of_rows(parts, arrays, 0, 4 * rows, 4 * rows, held), sems)
    copies[0].wait()
    for chunk in range(CHUNKS):
        for at in range(4):
            outer, low = place_of(inner, chunk, at // 2, at % 2)
            start = (4 * chunk + at) * rows
            left[:, start:start + rows] = held_slab[outer * LOW + low].T
    high, rest = halves(left[...])
    for copy in copies[1:]:
        copy.wait()
    both = dot(jnp.concatenate([high, rest], axis=0), held[:total, :])
    product[...] = both[:BW] + (both[BW:] + dot(high, held[total:, :]))


def project(inner, arrays, slab):
    full = arrays[0].shape[1]
    parts = [array.shape[0] // (4 * slab.shape[1]) for array in arrays[::2]]
    total = CHUNKS * 4 * slab.shape[1]
    return call(
        functools.partial(project_kernel, inner, parts), "project", [shape((BW, full))], pinned((*arrays, slab)), far=len(arrays) + 1,
        scratch=[pltpu.VMEM((BW, total), F32), pltpu.VMEM((2 * total, full), BF16), pltpu.VMEM(slab.shape, F32)],
        copies=2 * CHUNKS + 1, flops=6 * full * total * BW,
    )[0]


def change(inner, by_x, held, wide, slab, result):
    rows = slab.shape[1]
    delta = dot3_wide(held[...], wide[...])
    for chunk in range(CHUNKS):
        for by_y in range(2):
            outer, low_at = place_of(inner, chunk, by_x, by_y)
            start = (2 * chunk + by_y) * rows
            result[low_at] = slab[outer * LOW + low_at] - delta[start:start + rows, :]


def solve_kernel(inner, parts, own, other, diag_own, diag_other, corner_own, corner_other, *refs):
    arrays, refs = refs[:len(parts) * 2], refs[len(parts) * 2:]
    slab, away, wide, held_diag_own, held_diag_other, held_own, held_other, held, held_slab, sems = refs
    panels, width, _ = diag_own.shape
    pairs = pairs_of(panels)
    rows = slab.shape[1]
    diags = start_copies(
        [(far.at[p], near.at[p]) for p in range(panels) for far, near in ((diag_own, held_diag_own), (diag_other, held_diag_other))], sems
    )
    copies = start_copies(
        [(corner_own, held_own), (corner_other, held_other), (slab, held_slab)]
        + copies_of_rows(parts, arrays, 2 * rows, 2 * rows, 4 * rows, held), sems, 2 * panels
    )
    values = [(own[:, p * width:(p + 1) * width] + other[:, p * width:(p + 1) * width]).T for p in range(panels)]
    scaled = inverses(held_diag_own, held_diag_other, diags)
    for p in reversed(range(panels)):
        cut = slice(p * width, (p + 1) * width)
        solved = jnp.concatenate(halves(dot3_wide(scaled[p], jnp.concatenate(halves(values[p]), axis=1))), axis=1)
        wide[cut, :] = solved
        if p == panels - 1:
            copies[0].wait()
            copies[1].wait()
        for at, (i, q) in enumerate(pairs):
            if q == p:
                values[i] = values[i] - dot3_wide(jnp.concatenate(halves(held_own[at] + held_other[at]), axis=0), solved)
    for copy in copies[2:]:
        copy.wait()
    change(inner, 1, held, wide, held_slab, away)


def column_of(outer):
    return pl.ds(pl.multiple_of(outer * BW, BW), BW)


def copies_to_result(extra, half, column, result):
    rows = half.shape[1] // extra
    return [
        (half.at[low, e * rows:(e + 1) * rows, :], result.at[(e * LOW + low) * rows:(e * LOW + low + 1) * rows, column])
        for low in range(LOW) for e in range(extra)
    ]


def keep_kernel(inner, parts, extra, wide, *refs):
    arrays, (slab, result, keep, held, held_slab, sems) = refs[:len(parts) * 2], refs[len(parts) * 2:]
    rows = slab.shape[1]
    copies = start_copies([(slab, held_slab)] + copies_of_rows(parts, arrays, 0, 2 * rows, 4 * rows, held), sems)
    for copy in copies:
        copy.wait()
    change(inner, 0, held, wide, held_slab, keep)
    outer = lax.axis_index("row") // inner
    for copy in start_copies(copies_to_result(extra, keep, column_of(outer), result), sems, len(copies)):
        copy.wait()


def place_kernel(inner, extra, begun, back, result, sems):
    outer = lax.axis_index("row") // inner
    for copy in start_copies(copies_to_result(extra, back, column_of(1 - outer), result), sems):
        copy.wait()


def on_device(rows, cols, vectors, reflectors, owner_list, slot_list):
    inner = rows // 2
    extra = cols // LOW
    local_rows = vectors.shape[0] // cols
    panels = reflectors.shape[0]

    def at(row, col):
        return row * cols + col

    def send(value, change_of):
        perm = [(at(r, c), at(*change_of(r, c))) for r in range(rows) for c in range(cols)]
        return lax.ppermute(value, ("row", "col"), perm)

    def by_z(step):
        return lambda r, c: (r, c ^ (2 * step))

    def by_first(r, c):
        return (r, c ^ 1) if (r % inner) % 2 == 0 else ((r + inner) % rows, c)

    def by_second(r, c):
        return (r, c ^ 1) if (r % inner) % 2 == 1 else ((r + inner) % rows, c)

    def after(value, *others):
        return lax.optimization_barrier((value, *others))[0]

    own = reflectors
    if extra > 1:
        groups = [[e * LOW + low for e in range(extra)] for low in range(LOW)]
        own = lax.all_gather(own, "col", axis=1, tiled=True, axis_index_groups=groups)
    start = [own, send(own, by_z(1)), send(own, by_z(2))]
    start.append(send(start[2], by_z(1)))
    first = [send(piece, by_first) for piece in start]
    second = [send(piece, by_second) for piece in start]
    both = [send(piece, by_second) for piece in first]

    vectors = after(vectors, start[1], start[2], first[0], second[0])
    spread = lax.all_to_all(vectors.reshape(cols, local_rows, -1), "col", split_axis=0, concat_axis=0, tiled=True)
    ordered = reorder(spread, owner_list, slot_list)
    groups = [[at(o * inner + i, c) for o in range(2) for c in range(cols)] for i in range(inner)]
    slab = lax.all_to_all(ordered, ("row", "col"), split_axis=0, concat_axis=0, tiled=True, axis_index_groups=groups)
    slab = slab.reshape(2, extra, LOW, local_rows, BW).transpose(0, 2, 1, 3, 4)
    slab = slab.reshape(2 * LOW, extra * local_rows, BW)

    pieces = [(start[chunk], first[chunk], second[chunk], both[chunk]) for chunk in range(CHUNKS)]
    diag_blocks, corner_blocks = diag_pairs(panels), pairs_of(panels)
    diag, corner, high_a, low_a = gram(inner, sum(pieces[:-1], ()), None, (diag_blocks, corner_blocks), ordered)
    diag, corner, high_b, low_b = gram(inner, pieces[-1], (diag, corner), (diag_blocks, corner_blocks))
    arrays, parts = (high_a, low_a, high_b, low_b), (CHUNKS - 1, 1)
    def over_inner(value, bit):
        return send(value, lambda r, c: (r ^ bit, c))

    bits = [1 << k for k in range(inner.bit_length() - 1)]
    for bit in bits[:-1]:
        diag, corner = (value + over_inner(value, bit) for value in (diag, corner))
    diag_other = over_inner(diag, bits[-1])
    product = project(inner, arrays, slab)
    for bit in bits[:-1]:
        product = product + over_inner(product, bit)
    full, half_rows, block = product.shape[1], 2 * slab.shape[1], shape((LOW,) + slab.shape[1:])
    half_held = [pltpu.VMEM((2 * CHUNKS * half_rows, full), BF16), pltpu.VMEM(slab.shape, F32)]
    away, wide = call(
        functools.partial(solve_kernel, inner, parts), "solve", [block, shape((full, 2 * BW), BF16)],
        (product, over_inner(product, bits[-1]), *pinned((diag, diag_other, corner, over_inner(corner, bits[-1]))), *pinned((*arrays, slab))),
        far=len(arrays) + 5, copies=2 * panels + 2 * CHUNKS + 3,
        scratch=[pltpu.VMEM(diag.shape, F32)] * 2 + [pltpu.VMEM(corner.shape, F32)] * 2 + half_held, flops=8 * 10**9, mib=32,
    )
    back = send(away, lambda r, c: ((r + inner) % rows, c))
    begun, = call(
        functools.partial(keep_kernel, inner, parts, extra), "keep", [shape(vectors.shape)], (wide, *pinned((*arrays, slab))),
        far=len(arrays) + 1, far_outs=1, copies=2 * CHUNKS + 1 + LOW * extra, scratch=[pltpu.VMEM(block.shape, F32)] + half_held,
        flops=10**9,
    )
    result, = call(
        functools.partial(place_kernel, inner, extra), "place", [shape(vectors.shape)], (*pinned((begun,)), back), far=2, far_outs=1,
        copies=LOW * extra, aliases={0: 0},
    )
    return result


def solution(mesh):
    return jax.shard_map(
        functools.partial(on_device, mesh.shape["row"], mesh.shape["col"]),
        mesh=mesh,
        in_specs=(P("row", "col"), P(None, ("row", "col"), None), P(), P()),
        out_specs=P("row", "col"),
        check_vma=False,
    )
```

```python
import functools

import jax
import jax.numpy as jnp
from jax import lax
from jax.experimental import pallas as pl
from jax.experimental.pallas import tpu as pltpu
from jax.sharding import PartitionSpec as P

BW = 128
BLK_DEV = 2
LOW = 8
CHUNKS = 4
F32, BF16 = jnp.float32, jnp.bfloat16


def vmem(count):
    return [pl.BlockSpec(memory_space=pltpu.VMEM)] * count


def smem(count):
    return [pl.BlockSpec(memory_space=pltpu.SMEM)] * count


def shape(dims, kind=F32):
    return jax.ShapeDtypeStruct(tuple(dims), kind)


def call(body, name, outs, inputs, scratch=(), scalars=0, far=0, far_outs=0, copies=0, aliases=None, flops=0, mib=16):
    near = len(inputs) - scalars - far
    any_space = pl.BlockSpec(memory_space=pl.ANY)
    return pl.pallas_call(
        body,
        out_shape=tuple(outs[:len(outs) - far_outs]) + tuple(pltpu.HBM(out.shape, out.dtype) for out in outs[len(outs) - far_outs:]),
        in_specs=smem(scalars) + vmem(near) + [any_space] * far,
        out_specs=tuple(vmem(len(outs) - far_outs) + [any_space] * far_outs),
        scratch_shapes=list(scratch) + ([pltpu.SemaphoreType.DMA((copies,))] if copies else []),
        input_output_aliases=aliases or {},
        compiler_params=pltpu.CompilerParams(vmem_limit_bytes=mib * 1024 * 1024),
        cost_estimate=pl.CostEstimate(flops=flops, bytes_accessed=4 * 1024 * 1024, transcendentals=0),
        name=name,
    )(*inputs)


def pinned(arrays):
    return [pltpu.with_memory_space_constraint(array, pltpu.HBM) for array in arrays]


def start_copies(pairs, sems, base=0):
    copies = [pltpu.make_async_copy(src, dst, sems.at[base + at]) for at, (src, dst) in enumerate(pairs)]
    for copy in copies:
        copy.start()
    return copies


def halves(value):
    high = value.astype(BF16)
    return high, (value - high.astype(F32)).astype(BF16)


def dot(left, right):
    return jnp.dot(left, right, preferred_element_type=F32)


def dot3(left, right):
    rows = left[0].shape[0]
    both = dot(jnp.concatenate(left, axis=0), right[0])
    return both[:rows] + (both[rows:] + dot(left[0], right[1]))


def dot3_wide(left, wide):
    rows = left.shape[0] // 2
    full = dot(left, wide)
    return full[:rows, :BW] + (full[:rows, BW:] + full[rows:, :BW])


def pairs_of(panels):
    return [(p, q) for p in range(panels) for q in range(p + 1, panels)]


def reorder_kernel(half, owner_list, slot_list, spread, ordered, owner, slot, held, sems):
    copies = start_copies([(owner_list, owner), (slot_list, slot), (spread, held)], sems)
    for copy in copies:
        copy.wait()

    def move(block, carry):
        place = slot[block] * half + owner[block]
        parity = block % BLK_DEV

        @pl.when(parity == 0)
        def _():
            ordered[place] = held[block // BLK_DEV, :, :BW]

        @pl.when(parity == 1)
        def _():
            ordered[place] = held[block // BLK_DEV, :, BW:]

        return carry

    lax.fori_loop(0, ordered.shape[0], move, 0)


def reorder(spread, owner_list, slot_list):
    cols, rows, _ = spread.shape
    outs = [shape((cols * BLK_DEV, rows, BW))]
    scratch = [pltpu.SMEM(owner_list.shape, jnp.int32), pltpu.SMEM(slot_list.shape, jnp.int32), pltpu.VMEM(spread.shape, F32)]
    return call(
        functools.partial(reorder_kernel, cols), "reorder", outs, (*pinned((owner_list, slot_list)), spread), far=3, copies=3, scratch=scratch
    )[0]


def share_kernel(vectors, *refs):
    outs, sems = refs[:-1], refs[-1]
    z = lax.axis_index("col") // 2
    rows = outs[0].shape[0]
    pairs = []
    for at, out in enumerate(outs):
        start = pl.multiple_of(jnp.bitwise_xor(z, at + 1) * rows, rows)
        pairs.append((vectors.at[pl.ds(start, rows), :], out))
    for copy in start_copies(pairs, sems):
        copy.wait()


def halves_of(vectors, received, odd_half):
    col = lax.axis_index("col")
    rows = received[0].shape[0] // 2
    side = jnp.bitwise_xor(col % 2, odd_half) * rows
    refs = [vectors.at[pl.ds(pl.multiple_of((col // 2) * 2 * rows + side, rows), rows), :]]
    return refs + [ref.at[pl.ds(pl.multiple_of(side, rows), rows), :] for ref in received]


def turn_kernel(vectors, *refs):
    received, out, sems = refs[:-2], refs[-2], refs[-1]
    for copy in start_copies([(half, out.at[at]) for at, half in enumerate(halves_of(vectors, received, 1))], sems):
        copy.wait()


def place_blocks(half, owner, slot, held, ordered):
    def move(block, carry):
        place = slot[block] * half + owner[block]
        parity = block % BLK_DEV

        @pl.when(parity == 0)
        def _():
            ordered[place] = held[block // BLK_DEV, :, :BW]

        @pl.when(parity == 1)
        def _():
            ordered[place] = held[block // BLK_DEV, :, BW:]

        return carry

    lax.fori_loop(0, ordered.shape[0], move, 0)


def gather_kernel(half, owner_list, slot_list, vectors, *refs):
    received, (turned, ordered, owner, slot, held, sems) = refs[:-6], refs[-6:]
    col = lax.axis_index("col")
    z, y = col // 2, col % 2
    pairs = [(owner_list, owner), (slot_list, slot)]
    for at, part in enumerate(halves_of(vectors, received, 0)):
        source = jnp.bitwise_xor(z, at) * 2
        pairs += [(part, held.at[source + y]), (turned.at[at], held.at[source + 1 - y])]
    for copy in start_copies(pairs, sems):
        copy.wait()
    place_blocks(half, owner, slot, held, ordered)


def spread_by_steps(vectors, owner_list, slot_list, send, by_z, by_y, cols):
    rows, width = vectors.shape
    part, steps = rows // cols, cols // 2
    sent = call(share_kernel, "share", [shape((2 * part, width))] * (steps - 1), pinned((vectors,)), far=1, copies=steps - 1)
    received = [send(value, by_z(at + 1)) for at, value in enumerate(sent)]
    turned = call(
        turn_kernel, "turn", [shape((steps, part, width))], pinned((vectors, *received)), far=steps, copies=steps
    )[0]
    turned = send(turned, by_y)
    scratch = [pltpu.SMEM(owner_list.shape, jnp.int32), pltpu.SMEM(slot_list.shape, jnp.int32), pltpu.VMEM((cols, part, width), F32)]
    return call(
        functools.partial(gather_kernel, cols), "gather", [shape((cols * BLK_DEV, part, BW))],
        pinned((owner_list, slot_list, vectors, *received, turned)), far=steps + 3, copies=2 + 2 * steps, scratch=scratch,
    )[0]


def is_odd(inner):
    return (lax.axis_index("row") % inner) % 2


def gram_kernel(inner, count, summed, wanted, *refs):
    pieces, refs = refs[:4 * count], refs[4 * count:]
    before, refs = (refs[:len(wanted)], refs[len(wanted):]) if summed else ((), refs)
    outs, (high_out, low_out, staged, high, low, high_t, low_t, *held, sems) = refs[:len(wanted)], refs[len(wanted):]
    panels, rows, width = pieces[0].shape
    odd = is_odd(inner)
    places = (0, jnp.where(odd == 0, 1, 2), jnp.where(odd == 0, 2, 1), 3)
    arriving = start_copies([(piece, staged.at[at]) for at, piece in enumerate(pieces)], sems)
    base = 4 * count
    sums = start_copies(list(zip(before, held)), sems, base)
    for at, copy in enumerate(arriving):
        copy.wait()
        cut = pl.ds(pl.multiple_of((at // 4 * 4 + places[at % 4]) * rows, rows), rows)
        for p in range(panels):
            top, rest = halves(staged[at, p])
            high[cut, p * width:(p + 1) * width] = top
            low[cut, p * width:(p + 1) * width] = rest
    leaving = start_copies([(high, high_out), (low, low_out)], sems, base + 2)
    for copy in sums:
        copy.wait()
    cuts = [slice(p * width, (p + 1) * width) for p in range(panels)]
    for cut in cuts:
        high_t[cut, :] = high[:, cut].T
        low_t[cut, :] = low[:, cut].T
    base += 4
    for kind, blocks in enumerate(wanted):
        for at, (p, q) in enumerate(blocks):
            value = dot3((high_t[cuts[p], :], low_t[cuts[p], :]), (high[:, cuts[q]], low[:, cuts[q]]))
            held[kind][at] = value + held[kind][at] if summed else value
            leaving += start_copies([(held[kind].at[at], outs[kind].at[at])], sems, base)
            base += 1
    for copy in leaving:
        copy.wait()


def diag_pairs(panels):
    return [(p, p) for p in range(panels)]


def gram(inner, pieces, before, wanted, after=None):
    panels, rows, width = pieces[0].shape
    count = len(pieces) // 4
    total, full = len(pieces) * rows, panels * width
    blocks = [shape((len(pairs), width, width)) for pairs in wanted]
    outs = blocks + [shape((total, full), BF16), shape((total, full), BF16)]
    far = list(pieces) + pinned(before or ())
    used = len(far)
    if after is not None:
        far.append(after)

    def body(*refs):
        gram_kernel(inner, count, before is not None, wanted, *refs[:used], *refs[len(far):])

    number = sum(len(pairs) for pairs in wanted)
    return call(
        body, "gram", outs, far, far=len(far), far_outs=len(outs), copies=4 * count + 4 + number,
        scratch=[
            pltpu.VMEM((len(pieces), panels, rows, width), F32), pltpu.VMEM((total, full), BF16), pltpu.VMEM((total, full), BF16),
            pltpu.VMEM((full, total), BF16), pltpu.VMEM((full, total), BF16), *(pltpu.VMEM(block.shape, F32) for block in blocks),
        ],
        flops=6 * number * width * width * total, mib=32,
    )


def corner_kernel(panels, high_in, low_in, before, corner, high, low, held, sems):
    width = high.shape[1] // panels
    copies = start_copies([(high_in, high), (low_in, low), (before, held)], sems)
    for copy in copies[:2]:
        copy.wait()
    cuts = [slice(p * width, (p + 1) * width) for p in range(panels)]
    left = [(high[:, cut].T, low[:, cut].T) for cut in cuts[:-1]]
    copies[2].wait()
    leaving = []
    for at, (p, q) in enumerate(pairs_of(panels)):
        held[at] += dot3(left[p], (high[:, cuts[q]], low[:, cuts[q]]))
        leaving += start_copies([(held.at[at], corner.at[at])], sems, 3 + at)
    for copy in leaving:
        copy.wait()


def corners(panels, parts, before):
    total, full = parts[0].shape
    count, width, _ = before.shape
    return call(
        functools.partial(corner_kernel, panels), "corner", [shape(before.shape)], pinned((*parts, before)), far=3, far_outs=1,
        copies=3 + count, scratch=[pltpu.VMEM((total, full), BF16), pltpu.VMEM((total, full), BF16), pltpu.VMEM(before.shape, F32)],
        flops=6 * count * width * width * total,
    )[0]


def inverses(own, other, copies):
    panels, order, _ = own.shape
    row = lax.broadcasted_iota(jnp.int32, (order, order), 0)
    col = lax.broadcasted_iota(jnp.int32, (order, order), 1)
    apart = jnp.bitwise_xor(row, col)
    strict, edges, scale = [], [], []
    for p in range(panels):
        copies[2 * p].wait()
        copies[2 * p + 1].wait()
        gram_sum = own[p] + other[p]
        half = jnp.where(apart == 0, 0.5 * gram_sum, 0.0)
        by_row = 1.0 / jnp.sum(half, axis=1, keepdims=True)
        by_col = 1.0 / jnp.sum(half, axis=0, keepdims=True)
        strict.append(jnp.where(row < col, gram_sum * by_row, 0.0))
        edges.append(halves(strict[-1]))
        scale.append(by_col)

    def stacked(value):
        high, rest = halves(value)
        return jnp.concatenate([high.astype(F32), rest.astype(F32)], axis=0).astype(BF16)

    def multiply(left, right):
        rows = left.shape[0]
        if rows >= 16:
            return dot3(halves(left), right)
        both = stacked(left)
        full = dot(both, right[0])
        return full[:rows] + (full[rows:] + dot(both, right[1])[:rows])

    def inside(size):
        return jnp.where(apart < size, 1.0, 0.0)

    def widen(value):
        size = value.shape[0]
        if size < 16:
            return halves(jnp.concatenate([value] * (order // size), axis=0) * inside(size))
        mask = inside(size).astype(BF16)
        return tuple(jnp.concatenate([part] * (order // size), axis=0) * mask for part in halves(value))

    size = 8
    mask = inside(size)
    small_row = lax.broadcasted_iota(jnp.int32, (size, order), 0)
    small_col = lax.broadcasted_iota(jnp.int32, (size, order), 1)
    identity = jnp.where(small_row == small_col % size, 1.0, 0.0)
    full = [value * -mask for value in strict]
    power = [sum(value[k:k + size] for k in range(0, order, size)) for value in full]
    accum = [identity + value for value in power]
    power = [multiply(value, halves(wide)) for value, wide in zip(power, full)]
    both = [multiply(jnp.concatenate([value, extra], axis=0), widen(extra)) for value, extra in zip(accum, power)]
    accum = [value + extra[:size] for value, extra in zip(accum, both)]
    accum = [value + multiply(value, widen(extra[size:])) for value, extra in zip(accum, both)]
    while size < order:
        between = (inside(2 * size) - inside(size)).astype(BF16)
        lane = lax.broadcasted_iota(jnp.int32, (size, order), 1)
        even = (lane // size) % 2 == 0
        uppers = [jnp.where(even, value, 0.0) for value in accum]
        part = [multiply(value, (edge[0] * between, edge[1] * between)) for value, edge in zip(uppers, edges)]
        part = [multiply(edge, widen(value)) for edge, value in zip(part, accum)]
        accum = [
            jnp.concatenate([upper - edge, jnp.where(even, 0.0, value)], axis=0) for upper, edge, value in zip(uppers, part, accum)
        ]
        size *= 2
    return [jnp.concatenate(halves(value * by_col), axis=0) for value, by_col in zip(accum, scale)]


def place_of(inner, chunk, by_x, by_y):
    row, col = lax.axis_index("row"), lax.axis_index("col")
    return jnp.bitwise_xor(row // inner, by_x), jnp.bitwise_xor(col % LOW, chunk * 2 + by_y)


def copies_of_rows(parts, arrays, first, count, stride, held):
    pairs = []
    for k in range(2):
        at = k * CHUNKS * count
        for part, chunks in enumerate(parts):
            for chunk in range(chunks):
                pairs.append((arrays[2 * part + k].at[chunk * stride + first:chunk * stride + first + count, :], held.at[at:at + count, :]))
                at += count
    return pairs


def project_kernel(inner, parts, *refs):
    arrays, (slab, product, left, held, held_slab, sems) = refs[:len(parts) * 2], refs[len(parts) * 2:]
    rows = slab.shape[1]
    total = CHUNKS * 4 * rows
    copies = start_copies([(slab, held_slab)] + copies_of_rows(parts, arrays, 0, 4 * rows, 4 * rows, held), sems)
    copies[0].wait()
    for chunk in range(CHUNKS):
        for at in range(4):
            outer, low = place_of(inner, chunk, at // 2, at % 2)
            start = (4 * chunk + at) * rows
            left[:, start:start + rows] = held_slab[outer * LOW + low].T
    high, rest = halves(left[...])
    for copy in copies[1:]:
        copy.wait()
    both = dot(jnp.concatenate([high, rest], axis=0), held[:total, :])
    product[...] = both[:BW] + (both[BW:] + dot(high, held[total:, :]))


def project(inner, arrays, slab):
    full = arrays[0].shape[1]
    parts = [array.shape[0] // (4 * slab.shape[1]) for array in arrays[::2]]
    total = CHUNKS * 4 * slab.shape[1]
    return call(
        functools.partial(project_kernel, inner, parts), "project", [shape((BW, full))], pinned((*arrays, slab)), far=len(arrays) + 1,
        scratch=[pltpu.VMEM((BW, total), F32), pltpu.VMEM((2 * total, full), BF16), pltpu.VMEM(slab.shape, F32)],
        copies=2 * CHUNKS + 1, flops=6 * full * total * BW,
    )[0]


def change(inner, by_x, held, wide, slab, result):
    rows = slab.shape[1]
    delta = dot3_wide(held[...], wide[...])
    for chunk in range(CHUNKS):
        for by_y in range(2):
            outer, low_at = place_of(inner, chunk, by_x, by_y)
            start = (2 * chunk + by_y) * rows
            result[low_at] = slab[outer * LOW + low_at] - delta[start:start + rows, :]


def solve_kernel(inner, parts, own, other, diag_own, diag_other, corner_own, corner_other, *refs):
    arrays, refs = refs[:len(parts) * 2], refs[len(parts) * 2:]
    slab, away, wide, held_diag_own, held_diag_other, held_own, held_other, held, held_slab, sems = refs
    panels, width, _ = diag_own.shape
    pairs = pairs_of(panels)
    rows = slab.shape[1]
    diags = start_copies(
        [(far.at[p], near.at[p]) for p in range(panels) for far, near in ((diag_own, held_diag_own), (diag_other, held_diag_other))], sems
    )
    copies = start_copies(
        [(corner_own, held_own), (corner_other, held_other), (slab, held_slab)]
        + copies_of_rows(parts, arrays, 2 * rows, 2 * rows, 4 * rows, held), sems, 2 * panels
    )
    values = [(own[:, p * width:(p + 1) * width] + other[:, p * width:(p + 1) * width]).T for p in range(panels)]
    scaled = inverses(held_diag_own, held_diag_other, diags)
    for p in reversed(range(panels)):
        cut = slice(p * width, (p + 1) * width)
        solved = jnp.concatenate(halves(dot3_wide(scaled[p], jnp.concatenate(halves(values[p]), axis=1))), axis=1)
        wide[cut, :] = solved
        if p == panels - 1:
            copies[0].wait()
            copies[1].wait()
        for at, (i, q) in enumerate(pairs):
            if q == p:
                values[i] = values[i] - dot3_wide(jnp.concatenate(halves(held_own[at] + held_other[at]), axis=0), solved)
    for copy in copies[2:]:
        copy.wait()
    change(inner, 1, held, wide, held_slab, away)


def column_of(outer):
    return pl.ds(pl.multiple_of(outer * BW, BW), BW)


def copies_to_result(extra, half, column, result):
    rows = half.shape[1] // extra
    return [
        (half.at[low, e * rows:(e + 1) * rows, :], result.at[(e * LOW + low) * rows:(e * LOW + low + 1) * rows, column])
        for low in range(LOW) for e in range(extra)
    ]


def keep_kernel(inner, parts, extra, wide, *refs):
    arrays, (slab, result, keep, held, held_slab, sems) = refs[:len(parts) * 2], refs[len(parts) * 2:]
    rows = slab.shape[1]
    copies = start_copies([(slab, held_slab)] + copies_of_rows(parts, arrays, 0, 2 * rows, 4 * rows, held), sems)
    for copy in copies:
        copy.wait()
    change(inner, 0, held, wide, held_slab, keep)
    outer = lax.axis_index("row") // inner
    for copy in start_copies(copies_to_result(extra, keep, column_of(outer), result), sems, len(copies)):
        copy.wait()


def place_kernel(inner, extra, begun, back, result, sems):
    outer = lax.axis_index("row") // inner
    for copy in start_copies(copies_to_result(extra, back, column_of(1 - outer), result), sems):
        copy.wait()


def on_device(rows, cols, vectors, reflectors, owner_list, slot_list):
    inner = rows // 2
    extra = cols // LOW
    local_rows = vectors.shape[0] // cols
    panels = reflectors.shape[0]

    def at(row, col):
        return row * cols + col

    def send(value, change_of):
        perm = [(at(r, c), at(*change_of(r, c))) for r in range(rows) for c in range(cols)]
        return lax.ppermute(value, ("row", "col"), perm)

    def by_z(step):
        return lambda r, c: (r, c ^ (2 * step))

    def by_first(r, c):
        return (r, c ^ 1) if (r % inner) % 2 == 0 else ((r + inner) % rows, c)

    def by_second(r, c):
        return (r, c ^ 1) if (r % inner) % 2 == 1 else ((r + inner) % rows, c)

    def after(value, *others):
        return lax.optimization_barrier((value, *others))[0]

    own = reflectors
    if extra > 1:
        groups = [[e * LOW + low for e in range(extra)] for low in range(LOW)]
        own = lax.all_gather(own, "col", axis=1, tiled=True, axis_index_groups=groups)
    start = [own, send(own, by_z(1)), send(own, by_z(2))]
    start.append(send(start[2], by_z(1)))
    if extra == 1:
        ordered = spread_by_steps(vectors, owner_list, slot_list, send, by_z, lambda r, c: (r, c ^ 1), cols)
    else:
        spread = lax.all_to_all(vectors.reshape(cols, local_rows, -1), "col", split_axis=0, concat_axis=0, tiled=True)
        ordered = reorder(spread, owner_list, slot_list)
    first = [send(piece, by_first) for piece in start]
    second = [send(piece, by_second) for piece in [after(x, ordered) if k in (1, 2, 3) else x for k, x in enumerate(start)]]
    both = [send(piece, by_second) for piece in first]

    groups = [[at(o * inner + i, c) for o in range(2) for c in range(cols)] for i in range(inner)]
    slab = lax.all_to_all(ordered, ("row", "col"), split_axis=0, concat_axis=0, tiled=True, axis_index_groups=groups)
    slab = slab.reshape(2, extra, LOW, local_rows, BW).transpose(0, 2, 1, 3, 4)
    slab = slab.reshape(2 * LOW, extra * local_rows, BW)

    pieces = [(start[chunk], first[chunk], second[chunk], both[chunk]) for chunk in range(CHUNKS)]
    diag_blocks, corner_blocks = diag_pairs(panels), pairs_of(panels)
    diag, corner, high_a, low_a = gram(inner, sum(pieces[:-1], ()), None, (diag_blocks, corner_blocks), ordered)
    diag, corner, high_b, low_b = gram(inner, pieces[-1], (diag, corner), (diag_blocks, corner_blocks))
    arrays, parts = (high_a, low_a, high_b, low_b), (CHUNKS - 1, 1)
    def over_inner(value, bit):
        return send(value, lambda r, c: (r ^ bit, c))

    bits = [1 << k for k in range(inner.bit_length() - 1)]
    for bit in bits[:-1]:
        diag, corner = (value + over_inner(value, bit) for value in (diag, corner))
    diag_other = over_inner(diag, bits[-1])
    product = project(inner, arrays, slab)
    for bit in bits[:-1]:
        product = product + over_inner(product, bit)
    full, half_rows, block = product.shape[1], 2 * slab.shape[1], shape((LOW,) + slab.shape[1:])
    half_held = [pltpu.VMEM((2 * CHUNKS * half_rows, full), BF16), pltpu.VMEM(slab.shape, F32)]
    away, wide = call(
        functools.partial(solve_kernel, inner, parts), "solve", [block, shape((full, 2 * BW), BF16)],
        (product, over_inner(product, bits[-1]), *pinned((diag,)), diag_other, *pinned((corner,)), over_inner(corner, bits[-1]), *pinned((*arrays, slab))),
        far=len(arrays) + 5, copies=2 * panels + 2 * CHUNKS + 3,
        scratch=[pltpu.VMEM(diag.shape, F32)] * 2 + [pltpu.VMEM(corner.shape, F32)] * 2 + half_held, flops=8 * 10**9, mib=32,
    )
    back = send(away, lambda r, c: ((r + inner) % rows, c))
    begun, = call(
        functools.partial(keep_kernel, inner, parts, extra), "keep", [shape(vectors.shape)], (wide, *pinned((*arrays, slab))),
        far=len(arrays) + 1, far_outs=1, copies=2 * CHUNKS + 1 + LOW * extra, scratch=[pltpu.VMEM(block.shape, F32)] + half_held,
        flops=10**9,
    )
    result, = call(
        functools.partial(place_kernel, inner, extra), "place", [shape(vectors.shape)], (*pinned((begun,)), back), far=2, far_outs=1,
        copies=LOW * extra, aliases={0: 0},
    )
    return result


def solution(mesh):
    return jax.shard_map(
        functools.partial(on_device, mesh.shape["row"], mesh.shape["col"]),
        mesh=mesh,
        in_specs=(P("row", "col"), P(None, ("row", "col"), None), P(), P()),
        out_specs=P("row", "col"),
        check_vma=False,
    )
```
